32 devices in a mesh: tmpl: 8 (over z, core), chan: 4 (over y, x).
Axes of the slice: x: 2, y: 2, z: 4, core: 2. Of those that a mesh axis runs over, the one named last changes fastest.
Arguments:
- data: bfloat16 [8, 96, 2304], P('tmpl', 'chan')
- templates: bfloat16 [2048, 96, 200], P('tmpl', 'chan')
- counts: int32 [8], P('tmpl'), may hold values from 32 to 256, as said below
- owners: int32 [3], replicated, may hold values from 0 to 7
Outputs:
- traces: float32 [2048, 3, 2048], P('tmpl', None, 'chan')
The draws below stay inside these ranges and needn't reach their ends.
Inputs may be any that keep to these rules, and one draw needn't show every extreme that they name: `counts`: every count is a multiple of 32; some index of tmpl holds exactly 256 live slots.
All inputs are finite; a program needn't handle non-finite values.
Results may differ from the reference program's by a relative error of at most 0.0041.
Values may be sent and summed in bfloat16 or wider, within the bound.
No kernel may reach another device: no remote copies, remote signals or barrier semaphores. Data moves between devices by JAX's collectives and lax.ppermute only.
A program may use at most 128 MiB of HBM per device.

```python
import math
import jax
import jax.numpy as jnp
from jax import lax

C = 96
W = 200
NB = 3
LO = 2048
K_CAP = 256
TB = 32
LB = 2304
KTOT = 2048
N_TMPL = 8


def draw_data(key, part):
    keys = jax.random.split(key, 3)
    shape = (N_TMPL, C, LB)
    base = jax.random.normal(keys[0], shape, jnp.float32)
    chan_scale = jnp.exp(jax.random.uniform(keys[1], (N_TMPL, C, 1), jnp.float32) * math.log(10.0))
    time_scale = jnp.exp(jax.random.uniform(keys[2], (N_TMPL, 1, LB), jnp.float32) * math.log(10.0))
    return (base * chan_scale * time_scale).astype(jnp.bfloat16)


def draw_templates(key, part):
    keys = jax.random.split(key, 3)
    shape = (KTOT, C, W)
    base = jax.random.normal(keys[0], shape, jnp.float32)
    row_scale = jnp.exp(jax.random.uniform(keys[1], (KTOT, C, 1), jnp.float32) * math.log(10.0))
    sample_scale = jnp.exp(jax.random.uniform(keys[2], (KTOT, 1, W), jnp.float32) * math.log(10.0))
    return (base * row_scale * sample_scale).astype(jnp.bfloat16)


def draw_counts(key, part):
    keys = jax.random.split(key, 2)
    shifts = jax.random.randint(keys[0], (N_TMPL,), 0, 4)
    units = jnp.right_shift(jnp.full((N_TMPL,), K_CAP // TB, jnp.int32), shifts.astype(jnp.int32))
    fullest = jax.random.randint(keys[1], (), 0, N_TMPL)
    units = jnp.where(jnp.arange(N_TMPL, dtype=jnp.int32) == fullest, K_CAP // TB, units)
    return (units * TB).astype(jnp.int32)


def setup_inputs(seed: int = 0) -> dict:
    key_list = jax.random.split(jax.random.key(seed), 5)
    data = draw_data(jax.random.fold_in(key_list[4], 71), 0)
    templates = draw_templates(jax.random.fold_in(key_list[4], 71), 0)
    counts = draw_counts(jax.random.fold_in(key_list[4], 71), 0)
    owners = jax.random.randint(key_list[3], (NB,), 0, N_TMPL).astype(jnp.int32)
    return {"data": data, "templates": templates, "counts": counts, "owners": owners}


eps_value = 1e-06

def normalize_templates(templates):
    values = templates.astype(jnp.float32)
    spread = jnp.sqrt(lax.optimization_barrier(jnp.mean(values * values, axis=-1, keepdims=True)) + eps_value)
    scaled = (values / (spread * math.sqrt(values.shape[-1]))).astype(jnp.bfloat16)
    return scaled.reshape(values.shape[0], -1)

def scaled_windows(segment, window_len, lag_count):
    rows = segment.shape[0]
    length = segment.shape[1]
    period = length - 1
    tiled = jnp.tile(segment[:, :period], (1, window_len + 1))
    windows = tiled[:, :window_len * length].reshape(rows, window_len, length)[:, :, :lag_count].astype(jnp.float32)
    spread = jnp.sqrt(lax.optimization_barrier(jnp.mean(windows * windows, axis=1, keepdims=True)) + eps_value)
    scaled = (windows / (spread * math.sqrt(window_len))).astype(jnp.bfloat16)
    return scaled.reshape(-1, lag_count)

def reference(data, templates, counts, owners):
    normed = normalize_templates(templates)
    slots = jnp.arange(KTOT, dtype=jnp.int32)
    holder = slots // K_CAP
    live = slots % K_CAP < counts[holder]
    results = []
    for number in range(NB):
        segment = lax.dynamic_index_in_dim(data, owners[number], 0, keepdims=False)
        scaled = scaled_windows(segment, W, LO)
        corr = jnp.dot(normed, scaled, preferred_element_type=jnp.float32)
        results.append(jnp.where(live[:, None], corr, jnp.float32(0.0)))
    return jnp.stack(results, axis=1)
```

```python
import functools
import math

import jax
import jax.numpy as jnp
from jax import lax
from jax.experimental import pallas as pl
from jax.experimental.pallas import tpu as pltpu
from jax.sharding import PartitionSpec as P

W = 200
NB = 3
LO = 2048
TB = 32
EPS = 1e-06
VMEM_LIMIT = 48 * 2**20


def inverse_norm(mean_square):
    return 1.0 / (jnp.sqrt(mean_square + EPS) * math.sqrt(W))


def template_kernel(tpl_ref, out_ref, scaled_ref):
    chans, _, slots = tpl_ref.shape
    for c in range(0, chans, 2):
        pair = []
        for k in (c, c + 1):
            values = tpl_ref[k].astype(jnp.float32)
            mean_square = jnp.sum(values * values, axis=0, keepdims=True) * (1.0 / W)
            pair.append(values * inverse_norm(mean_square))
        scaled_ref[c * W : (c + 2) * W, :] = jnp.concatenate(pair, 0).astype(jnp.bfloat16)
    depth = chans * W
    for at in range(0, depth, slots):
        size = min(slots, depth - at)
        out_ref[:, at : at + size] = scaled_ref[at : at + size, :].T


def normalize_templates(templates):
    slots, chans, _ = templates.shape
    return pl.pallas_call(
        template_kernel,
        out_shape=jax.ShapeDtypeStruct((slots, chans * W), jnp.bfloat16),
        scratch_shapes=[pltpu.VMEM((chans * W, slots), jnp.bfloat16)],
        compiler_params=pltpu.CompilerParams(vmem_limit_bytes=VMEM_LIMIT),
        cost_estimate=pl.CostEstimate(
            flops=4 * slots * chans * W, bytes_accessed=4 * slots * chans * W, transcendentals=0
        ),
        name="normalize_templates",
    )(jnp.transpose(templates, (1, 2, 0)))


def shift_left(x, amount):
    return pltpu.roll(x, x.shape[1] - amount, 1) if amount else x


def build_windows(segment, base_ref, win_ref, lags):
    chans, span = segment.shape
    sums = {1: segment * segment}
    for p in range(7):
        sums[2 << p] = sums[1 << p] + shift_left(sums[1 << p], 1 << p)
    total = sums[128] + shift_left(sums[64], 128) + shift_left(sums[8], 192)
    scale = inverse_norm(total[:, :lags] * (1.0 / W))
    for s in range(8):
        moved = shift_left(segment, s)
        for j in range(span // 128):
            base_ref[j, pl.ds(s, chans, stride=8), :] = moved[:, 128 * j : 128 * (j + 1)]
    for c in range(0, chans, 2):
        rows = []
        for k in (c, c + 1):
            base = jnp.concatenate(
                [base_ref[j, k * 8 : k * 8 + 8, :] for j in range(span // 128)], 1
            )
            row_scale = jnp.broadcast_to(scale[k : k + 1, :], (8, lags))
            wide = [shift_left(base, 8 * g)[:, : lags + 128] for g in range(16)]
            rows += [wide[g][:, :lags] * row_scale for g in range(16)]
            rows += [wide[g][:, 128:] * row_scale for g in range((W - 128) // 8)]
        win_ref[c * W : (c + 2) * W, :] = jnp.concatenate(rows, 0).astype(jnp.bfloat16)


def partial_kernel(lags, place_ref, tpl_ref, even_ref, odd_ref, order_ref, out_ref, base_ref, win_ref):
    del order_ref
    start = pl.multiple_of(place_ref[0] * lags, 128)

    def one_block(number, carry):
        code = place_ref[1 + number]
        slot = lax.div(code, 2)
        window = pl.ds(start, lags + 256)
        segment = jnp.where(
            lax.rem(code, 2) == 1,
            odd_ref[slot, :, window].astype(jnp.float32),
            even_ref[slot, :, window].astype(jnp.float32),
        )
        build_windows(segment, base_ref, win_ref, lags)
        out_ref[number] = jnp.dot(
            tpl_ref[: out_ref.shape[1], :], win_ref[...], preferred_element_type=jnp.float32
        ).astype(out_ref.dtype)
        return carry

    lax.fori_loop(0, NB, one_block, 0)


def partial_sums(rows, lags, dtype, place, normed, even, odd, order):
    depth = normed.shape[1]
    chans = even.shape[1]
    whole = pl.BlockSpec(memory_space=pltpu.VMEM)
    return pl.pallas_call(
        functools.partial(partial_kernel, lags),
        out_shape=jax.ShapeDtypeStruct((NB, rows, lags), dtype),
        in_specs=[
            pl.BlockSpec(memory_space=pltpu.SMEM),
            whole,
            whole,
            whole,
            pl.BlockSpec(memory_space=pl.ANY),
        ],
        scratch_shapes=[
            pltpu.VMEM(((lags + 256) // 128, chans * 8, 128), jnp.float32),
            pltpu.VMEM((depth, lags), jnp.bfloat16),
        ],
        compiler_params=pltpu.CompilerParams(vmem_limit_bytes=VMEM_LIMIT),
        cost_estimate=pl.CostEstimate(
            flops=2 * NB * rows * depth * lags,
            bytes_accessed=2 * rows * depth + 4 * NB * rows * lags,
            transcendentals=0,
        ),
        name="partial_sums",
    )(place, normed, even, odd, order)


def correlate(rows, slots, lags, n_chan, normed, even, odd, codes, count):
    me = lax.axis_index("chan")
    order = codes
    arrived = []
    for step in list(range(n_chan - 1, 0, -1)):
        place = jnp.concatenate([jnp.reshape(me ^ step, (1,)), codes])
        partial = partial_sums(rows, lags, jnp.bfloat16, place, normed, even, odd, order)
        order = partial
        arrived.append(lax.ppermute(partial, "chan", [(i, i ^ step) for i in range(n_chan)]))
    place = jnp.concatenate([jnp.reshape(me, (1,)), codes])
    total = partial_sums(rows, lags, jnp.float32, place, normed, even, odd, order)
    for part in arrived:
        total = total + part.astype(jnp.float32)
    live = lax.broadcasted_iota(jnp.int32, total.shape, 1) < count
    total = jnp.where(live, total, 0.0)
    return jnp.pad(total, ((0, 0), (0, slots - rows), (0, 0)))


def body(n_tmpl, n_chan, data, templates, counts, owners):
    slots = templates.shape[0]
    lags = LO // n_chan
    parts = [data]
    for step in range(2, n_tmpl, 2):
        parts.append(lax.ppermute(data, "tmpl", [(i, i ^ step) for i in range(n_tmpl)]))
    even = jnp.concatenate(parts, 0)
    odd = lax.ppermute(even, "tmpl", [(i, i ^ 1) for i in range(n_tmpl)])
    normed = normalize_templates(templates)
    codes = owners ^ lax.axis_index("tmpl")
    count = counts[0]
    sizes = []
    size = slots
    while size >= TB:
        sizes.insert(0, size)
        size //= 2
    choice = sum((count > size).astype(jnp.int32) for size in sizes[:-1])
    traces = lax.switch(
        choice,
        [functools.partial(correlate, size, slots, lags, n_chan) for size in sizes],
        normed,
        even,
        odd,
        codes,
        count,
    )
    return jnp.transpose(traces, (1, 0, 2))


def solution(mesh):
    placed = (P("tmpl", "chan", None), P("tmpl", "chan", None), P("tmpl"), P())
    return jax.shard_map(
        functools.partial(body, mesh.shape["tmpl"], mesh.shape["chan"]),
        mesh=mesh,
        in_specs=placed,
        out_specs=P("tmpl", None, "chan"),
        check_vma=False,
    )
```

```python
import functools
import math

import jax
import jax.numpy as jnp
from jax import lax
from jax.experimental import pallas as pl
from jax.experimental.pallas import tpu as pltpu
from jax.sharding import PartitionSpec as P

W = 200
NB = 3
LO = 2048
TB = 32
EPS = 1e-06
VMEM_LIMIT = 48 * 2**20


def inverse_norm(mean_square):
    return 1.0 / (jnp.sqrt(mean_square + EPS) * math.sqrt(W))


def template_kernel(tpl_ref, out_ref, scaled_ref):
    chans, _, slots = tpl_ref.shape
    for c in range(0, chans, 2):
        pair = []
        for k in (c, c + 1):
            values = tpl_ref[k].astype(jnp.float32)
            mean_square = jnp.sum(values * values, axis=0, keepdims=True) * (1.0 / W)
            pair.append(values * inverse_norm(mean_square))
        scaled_ref[c * W : (c + 2) * W, :] = jnp.concatenate(pair, 0).astype(jnp.bfloat16)
    depth = chans * W
    for at in range(0, depth, slots):
        size = min(slots, depth - at)
        out_ref[:, at : at + size] = scaled_ref[at : at + size, :].T


def normalize_templates(templates):
    slots, chans, _ = templates.shape
    return pl.pallas_call(
        template_kernel,
        out_shape=jax.ShapeDtypeStruct((slots, chans * W), jnp.bfloat16),
        scratch_shapes=[pltpu.VMEM((chans * W, slots), jnp.bfloat16)],
        compiler_params=pltpu.CompilerParams(vmem_limit_bytes=VMEM_LIMIT),
        cost_estimate=pl.CostEstimate(
            flops=4 * slots * chans * W, bytes_accessed=4 * slots * chans * W, transcendentals=0
        ),
        name="normalize_templates",
    )(jnp.transpose(templates, (1, 2, 0)))


def shift_left(x, amount):
    return pltpu.roll(x, x.shape[1] - amount, 1) if amount else x


def block_kernel(code_ref, even_ref, odd_ref, seg_ref, scale_ref):
    chans = even_ref.shape[1]
    lags = scale_ref.shape[2]
    for number in range(NB):
        code = code_ref[number]
        slot = lax.div(code, 2)
        segment = jnp.where(
            lax.rem(code, 2) == 1,
            odd_ref[slot].astype(jnp.float32),
            even_ref[slot].astype(jnp.float32),
        )
        seg_ref[number, :chans, :] = segment.astype(jnp.bfloat16)
        sums = {1: segment * segment}
        for p in range(7):
            sums[2 << p] = sums[1 << p] + shift_left(sums[1 << p], 1 << p)
        total = sums[128] + shift_left(sums[64], 128) + shift_left(sums[8], 192)
        scale_ref[number, :chans, :] = inverse_norm(total[:, :lags] * (1.0 / W))


def choose_blocks(codes, even, odd):
    _, chans, length = even.shape
    held = -(-chans // 8) * 8
    return pl.pallas_call(
        block_kernel,
        out_shape=(
            jax.ShapeDtypeStruct((NB, held, length), jnp.bfloat16),
            jax.ShapeDtypeStruct((NB, held, LO), jnp.float32),
        ),
        in_specs=[
            pl.BlockSpec(memory_space=pltpu.SMEM),
            pl.BlockSpec(memory_space=pltpu.VMEM),
            pl.BlockSpec(memory_space=pltpu.VMEM),
        ],
        compiler_params=pltpu.CompilerParams(vmem_limit_bytes=VMEM_LIMIT),
        cost_estimate=pl.CostEstimate(flops=10**10, bytes_accessed=10**8, transcendentals=0),
        name="choose_blocks",
    )(codes, even, odd)


def build_windows(at, held, chans, base_ref, scale_ref, win_ref):
    lags = win_ref.shape[1]
    tiles = base_ref.shape[0]
    scale = scale_ref[at * held : (at + 1) * held, :]
    for c in range(0, chans, 2):
        rows = []
        for k in (c, c + 1):
            line = (at * held + k) * 8
            base = jnp.concatenate([base_ref[j, line : line + 8, :] for j in range(tiles)], 1)
            row_scale = jnp.broadcast_to(scale[k : k + 1, :], (8, lags))
            wide = [shift_left(base, 8 * g)[:, : lags + 128] for g in range(16)]
            rows += [wide[g][:, :lags] * row_scale for g in range(16)]
            rows += [wide[g][:, 128:] * row_scale for g in range((W - 128) // 8)]
        win_ref[c * W : (c + 2) * W, :] = jnp.concatenate(rows, 0).astype(jnp.bfloat16)


def partial_kernel(chunks, n_add, write, place_ref, tpl_ref, seg_ref, scale_ref, *refs):
    adds, outs = refs[1 : 1 + n_add], refs[1 + n_add : -4]
    seg_now, scale_now, base_now, win_ref = refs[-4:]
    depth, lags = win_ref.shape
    held = seg_ref.shape[1]
    span = seg_now.shape[1]
    for index, number in enumerate(chunks):
        start = pl.multiple_of(place_ref[index] * lags, 128)
        lines = slice(index * held, (index + 1) * held)
        seg_now[lines, :] = seg_ref[number, :, pl.ds(start, span)].astype(jnp.float32)
        scale_now[lines, :] = scale_ref[number, :, pl.ds(start, lags)]
    segment = seg_now[...]
    for s in range(8):
        moved = shift_left(segment, s)
        for j in range(span // 128):
            base_now[j, pl.ds(s, segment.shape[0], stride=8), :] = moved[:, 128 * j : 128 * (j + 1)]
    for index in range(len(chunks)):
        build_windows(index, held, depth // W, base_now, scale_now, win_ref)
        product = jnp.dot(tpl_ref[...], win_ref[...], preferred_element_type=jnp.float32)
        write(index, product, adds, outs)


def partial_sums(chunks, write, outs, place, normed, segments, scales, adds=(), order=None):
    lags = outs[0].shape[-1]
    depth = normed.shape[1]
    held = segments.shape[1]
    whole = pl.BlockSpec(memory_space=pltpu.VMEM)
    order = place if order is None else order
    return pl.pallas_call(
        functools.partial(partial_kernel, chunks, len(adds), write),
        out_shape=outs,
        in_specs=[
            pl.BlockSpec(memory_space=pltpu.SMEM),
            whole,
            whole,
            whole,
            pl.BlockSpec(memory_space=pl.ANY),
        ]
        + [whole] * len(adds),
        scratch_shapes=[
            pltpu.VMEM((len(chunks) * held, lags + 256), jnp.float32),
            pltpu.VMEM((len(chunks) * held, lags), jnp.float32),
            pltpu.VMEM(((lags + 256) // 128, len(chunks) * held * 8, 128), jnp.float32),
            pltpu.VMEM((depth, lags), jnp.bfloat16),
        ],
        compiler_params=pltpu.CompilerParams(vmem_limit_bytes=VMEM_LIMIT),
        cost_estimate=pl.CostEstimate(flops=10**12, bytes_accessed=10**10, transcendentals=0),
        name="partial_sums",
    )(place, normed, segments, scales, order, *adds)


def write_plain(index, product, adds, outs):
    outs[0][index] = product.astype(outs[0].dtype)


def write_halves(index, product, adds, outs):
    half = outs[0].shape[1]
    outs[0][index] = product[:half].astype(jnp.bfloat16)
    outs[1][index] = product[half:].astype(jnp.bfloat16)


def write_added(at, index, product, adds, outs):
    half = product.shape[0] // 2
    here = adds[index][at].astype(jnp.float32)
    if index == 0:
        outs[0][:half] = product[:half].astype(jnp.bfloat16)
        outs[0][half:] = (product[half:] + here).astype(jnp.bfloat16)
    else:
        outs[1][:half] = (product[:half] + here).astype(jnp.bfloat16)
        outs[1][half:] = product[half:].astype(jnp.bfloat16)


def exchange(value, step, n_chan):
    return lax.ppermute(value, "chan", [(i, i ^ step) for i in range(n_chan)])


def two_steps(normed, segments, scales, lags):
    slots = normed.shape[0]
    me = lax.axis_index("chan")
    args = (normed, segments, scales)

    def message(count, rows):
        return jax.ShapeDtypeStruct((count, rows, lags), jnp.bfloat16)

    via_x, via_y = [], []
    order = None
    for chunks in ((0,), (1, 2)):
        out = (message(len(chunks), slots // 2),) * 2
        place = jnp.stack([me ^ 3] * len(chunks))
        upper, lower = partial_sums(chunks, write_halves, out, place, *args, order=order)
        order = lower
        via_x.append(exchange(upper, 1, 4))
        via_y.append(exchange(lower, 2, 4))
    arrived = []
    place = jnp.stack([me ^ 1, me ^ 2])
    for number in range(NB):
        part, at = (0, 0) if number == 0 else (1, number - 1)
        out = (jax.ShapeDtypeStruct((slots, lags), jnp.bfloat16),) * 2
        to_x, to_y = partial_sums(
            (number, number),
            functools.partial(write_added, at),
            out,
            place,
            *args,
            adds=(via_y[part], via_x[part]),
            order=order,
        )
        order = to_y
        arrived.append((exchange(to_x, 1, 4), exchange(to_y, 2, 4)))
    out = (jax.ShapeDtypeStruct((NB, slots, lags), jnp.float32),)
    (total,) = partial_sums(
        tuple(range(NB)), write_plain, out, jnp.stack([me] * NB), *args, order=order
    )
    return total, [jnp.stack([pair[side] for pair in arrived]) for side in range(2)]


def one_step(normed, segments, scales, lags, n_chan):
    slots = normed.shape[0]
    me = lax.axis_index("chan")
    every = tuple(range(NB))
    arrived = []
    order = None
    for step in range(n_chan - 1, -1, -1):
        dtype = jnp.bfloat16 if step else jnp.float32
        out = (jax.ShapeDtypeStruct((NB, slots, lags), dtype),)
        place = jnp.stack([me ^ step] * NB)
        (order,) = partial_sums(
            every, write_plain, out, place, normed, segments, scales, order=order
        )
        if step:
            arrived.append(exchange(order, step, n_chan))
    return order, arrived


def body(n_tmpl, n_chan, data, templates, counts, owners):
    lags = LO // n_chan
    parts = [data]
    for step in range(2, n_tmpl, 2):
        parts.append(lax.ppermute(data, "tmpl", [(i, i ^ step) for i in range(n_tmpl)]))
    normed = normalize_templates(templates)
    even, normed = lax.optimization_barrier((jnp.concatenate(parts, 0), normed))
    odd = lax.ppermute(even, "tmpl", [(i, i ^ 1) for i in range(n_tmpl)])
    codes = owners ^ lax.axis_index("tmpl")
    segments, scales = choose_blocks(codes, even, odd)
    if n_chan == 4:
        total, arrived = two_steps(normed, segments, scales, lags)
    else:
        total, arrived = one_step(normed, segments, scales, lags, n_chan)
    for part in arrived:
        total = total + part.astype(jnp.float32)
    live = lax.broadcasted_iota(jnp.int32, total.shape, 1) < counts[0]
    return jnp.transpose(jnp.where(live, total, 0.0), (1, 0, 2))


def solution(mesh):
    placed = (P("tmpl", "chan", None), P("tmpl", "chan", None), P("tmpl"), P())
    return jax.shard_map(
        functools.partial(body, mesh.shape["tmpl"], mesh.shape["chan"]),
        mesh=mesh,
        in_specs=placed,
        out_specs=P("tmpl", None, "chan"),
        check_vma=False,
    )
```

```python
import functools
import math

import jax
import jax.numpy as jnp
from jax import lax
from jax.experimental import pallas as pl
from jax.experimental.pallas import tpu as pltpu
from jax.sharding import PartitionSpec as P

W = 200
NB = 3
LO = 2048
TB = 32
EPS = 1e-06
VMEM_LIMIT = 48 * 2**20


def inverse_norm(mean_square):
    return 1.0 / (jnp.sqrt(mean_square + EPS) * math.sqrt(W))


def template_kernel(count_ref, tpl_ref, out_ref, scaled_ref):
    chans, _, slots = tpl_ref.shape
    live = lax.broadcasted_iota(jnp.int32, (1, slots), 1) < count_ref[0]
    for c in range(0, chans, 2):
        pair = []
        for k in (c, c + 1):
            values = tpl_ref[k].astype(jnp.float32)
            mean_square = jnp.sum(values * values, axis=0, keepdims=True) * (1.0 / W)
            pair.append(jnp.where(live, values * inverse_norm(mean_square), 0.0))
        scaled_ref[c * W : (c + 2) * W, :] = jnp.concatenate(pair, 0).astype(jnp.bfloat16)
    depth = chans * W
    for at in range(0, depth, slots):
        size = min(slots, depth - at)
        out_ref[:, at : at + size] = scaled_ref[at : at + size, :].T


def normalize_templates(counts, templates):
    slots, chans, _ = templates.shape
    return pl.pallas_call(
        template_kernel,
        out_shape=jax.ShapeDtypeStruct((slots, chans * W), jnp.bfloat16),
        in_specs=[
            pl.BlockSpec(memory_space=pltpu.SMEM),
            pl.BlockSpec(memory_space=pltpu.VMEM),
        ],
        scratch_shapes=[pltpu.VMEM((chans * W, slots), jnp.bfloat16)],
        compiler_params=pltpu.CompilerParams(vmem_limit_bytes=VMEM_LIMIT),
        cost_estimate=pl.CostEstimate(
            flops=4 * slots * chans * W, bytes_accessed=4 * slots * chans * W, transcendentals=0
        ),
        name="normalize_templates",
    )(counts, jnp.transpose(templates, (1, 2, 0)))


def shift_left(x, amount):
    return pltpu.roll(x, x.shape[1] - amount, 1) if amount else x


def block_kernel(code_ref, even_ref, odd_ref, seg_ref, scale_ref):
    chans = even_ref.shape[1]
    lags = scale_ref.shape[2]
    for number in range(NB):
        code = code_ref[number]
        slot = lax.div(code, 2)
        segment = jnp.where(
            lax.rem(code, 2) == 1,
            odd_ref[slot].astype(jnp.float32),
            even_ref[slot].astype(jnp.float32),
        )
        seg_ref[number, :chans, :] = segment.astype(jnp.bfloat16)
        sums = {1: segment * segment}
        for p in range(7):
            sums[2 << p] = sums[1 << p] + shift_left(sums[1 << p], 1 << p)
        total = sums[128] + shift_left(sums[64], 128) + shift_left(sums[8], 192)
        scale_ref[number, :chans, :] = inverse_norm(total[:, :lags] * (1.0 / W))


def choose_blocks(codes, even, odd):
    _, chans, length = even.shape
    held = -(-chans // 8) * 8
    return pl.pallas_call(
        block_kernel,
        out_shape=(
            jax.ShapeDtypeStruct((NB, held, length), jnp.bfloat16),
            jax.ShapeDtypeStruct((NB, held, LO), jnp.float32),
        ),
        in_specs=[
            pl.BlockSpec(memory_space=pltpu.SMEM),
            pl.BlockSpec(memory_space=pltpu.VMEM),
            pl.BlockSpec(memory_space=pltpu.VMEM),
        ],
        compiler_params=pltpu.CompilerParams(vmem_limit_bytes=VMEM_LIMIT),
        cost_estimate=pl.CostEstimate(flops=10**10, bytes_accessed=10**8, transcendentals=0),
        name="choose_blocks",
    )(codes, even, odd)


def build_windows(at, held, chans, base_ref, scale_ref, win_ref):
    lags = win_ref.shape[1]
    tiles = base_ref.shape[0]
    scale = scale_ref[at * held : (at + 1) * held, :]
    for c in range(0, chans, 2):
        rows = []
        for k in (c, c + 1):
            line = (at * held + k) * 8
            base = jnp.concatenate([base_ref[j, line : line + 8, :] for j in range(tiles)], 1)
            row_scale = jnp.broadcast_to(scale[k : k + 1, :], (8, lags))
            wide = [shift_left(base, 8 * g)[:, : lags + 128] for g in range(16)]
            rows += [wide[g][:, :lags] * row_scale for g in range(16)]
            rows += [wide[g][:, 128:] * row_scale for g in range((W - 128) // 8)]
        win_ref[c * W : (c + 2) * W, :] = jnp.concatenate(rows, 0).astype(jnp.bfloat16)


def partial_kernel(chunks, n_add, n_order, write, place_ref, tpl_ref, seg_ref, scale_ref, *refs):
    adds, outs = refs[:n_add], refs[n_add + n_order : -4]
    seg_now, scale_now, base_now, win_ref = refs[-4:]
    depth, lags = win_ref.shape
    held = seg_ref.shape[1]
    span = seg_now.shape[1]
    for index, number in enumerate(chunks):
        start = pl.multiple_of(place_ref[index] * lags, 128)
        lines = slice(index * held, (index + 1) * held)
        seg_now[lines, :] = seg_ref[number, :, pl.ds(start, span)].astype(jnp.float32)
        scale_now[lines, :] = scale_ref[number, :, pl.ds(start, lags)]
    segment = seg_now[...]
    for s in range(8):
        moved = shift_left(segment, s)
        for j in range(span // 128):
            base_now[j, pl.ds(s, segment.shape[0], stride=8), :] = moved[:, 128 * j : 128 * (j + 1)]
    for index in range(len(chunks)):
        build_windows(index, held, depth // W, base_now, scale_now, win_ref)
        product = jnp.dot(tpl_ref[...], win_ref[...], preferred_element_type=jnp.float32)
        write(index, product, adds, outs)


def partial_sums(chunks, write, outs, place, normed, segments, scales, adds=(), order=()):
    lags = outs[0].shape[-1]
    depth = normed.shape[1]
    held = segments.shape[1]
    whole = pl.BlockSpec(memory_space=pltpu.VMEM)
    return pl.pallas_call(
        functools.partial(partial_kernel, chunks, len(adds), len(order), write),
        out_shape=outs,
        in_specs=[
            pl.BlockSpec(memory_space=pltpu.SMEM),
            whole,
            whole,
            whole,
        ]
        + [whole] * len(adds)
        + [pl.BlockSpec(memory_space=pl.ANY)] * len(order),
        scratch_shapes=[
            pltpu.VMEM((len(chunks) * held, lags + 256), jnp.float32),
            pltpu.VMEM((len(chunks) * held, lags), jnp.float32),
            pltpu.VMEM(((lags + 256) // 128, len(chunks) * held * 8, 128), jnp.float32),
            pltpu.VMEM((depth, lags), jnp.bfloat16),
        ],
        compiler_params=pltpu.CompilerParams(vmem_limit_bytes=VMEM_LIMIT),
        cost_estimate=pl.CostEstimate(flops=10**12, bytes_accessed=10**10, transcendentals=0),
        name="partial_sums",
    )(place, normed, segments, scales, *adds, *order)


def write_plain(index, product, adds, outs):
    if len(outs) == 1:
        outs[0][index] = product.astype(outs[0].dtype)
    else:
        outs[index][...] = product.astype(outs[index].dtype)


def write_across(index, product, adds, outs):
    half = outs[0].shape[1]
    if index < outs[0].shape[0]:
        outs[0][index] = product[:half].astype(jnp.bfloat16)
        outs[1][index] = product[half:].astype(jnp.bfloat16)
    else:
        outs[2][...] = product.astype(jnp.bfloat16)


def write_added(at, index, product, adds, outs):
    half = product.shape[0] // 2
    here = adds[index][at].astype(jnp.float32)
    if index == 0:
        outs[0][:half] = product[:half].astype(jnp.bfloat16)
        outs[0][half:] = (product[half:] + here).astype(jnp.bfloat16)
    else:
        outs[1][:half] = (product[:half] + here).astype(jnp.bfloat16)
        outs[1][half:] = product[half:].astype(jnp.bfloat16)


def exchange(value, step, n_chan):
    return lax.ppermute(value, "chan", [(i, i ^ step) for i in range(n_chan)])


def two_steps(normed, segments, scales, lags):
    slots = normed.shape[0]
    me = lax.axis_index("chan")
    args = (normed, segments, scales)

    def message(*shape):
        return jax.ShapeDtypeStruct(shape + (lags,), jnp.bfloat16)

    upper, lower, far = partial_sums(
        (1, 2, 0),
        write_across,
        (message(2, slots // 2), message(2, slots // 2), message(slots)),
        jnp.stack([me ^ 3] * NB),
        *args,
    )
    via_x, via_y = exchange(upper, 1, 4), exchange(lower, 2, 4)
    straight = exchange(far, 3, 4)
    arrived = []
    place = jnp.stack([me ^ 1, me ^ 2])
    order = (far,)
    for number in range(NB):
        write, adds = write_plain, ()
        if number > 0:
            write, adds = functools.partial(write_added, number - 1), (via_y, via_x)
        to_x, to_y = partial_sums(
            (number, number), write, (message(slots),) * 2, place, *args, adds=adds, order=order
        )
        order = (to_y,)
        if number == 1:
            order += (straight,)
        if number == NB - 1:
            to_x, to_y, *first = lax.optimization_barrier((to_x, to_y, *arrived[0]))
            arrived[0] = tuple(first)
        arrived.append((exchange(to_x, 1, 4), exchange(to_y, 2, 4)))
    (total,) = partial_sums(
        tuple(range(NB)),
        write_plain,
        (jax.ShapeDtypeStruct((NB, slots, lags), jnp.float32),),
        jnp.stack([me] * NB),
        *args,
        order=order[:1],
    )
    arrived[0] += (straight,)
    return finish(total, arrived)


def finish_kernel(shares, total_ref, *refs):
    n_part = sum(shares)
    parts, out_ref, stage = refs[:n_part], refs[n_part], refs[n_part + 1]
    held = refs[n_part + 2 : 2 * n_part + 2]
    semaphores = refs[2 * n_part + 2 :]
    arriving = [pltpu.make_async_copy(*trio) for trio in zip(parts, held, semaphores)]
    for copy in arriving:
        copy.start()
    leaving = []
    at = 0
    for number, share in enumerate(shares):
        value = total_ref[number]
        for index in range(at, at + share):
            arriving[index].wait()
            value = value + held[index][...].astype(jnp.float32)
        at += share
        stage[number] = value
        leaving.append(
            pltpu.make_async_copy(
                stage.at[number], out_ref.at[number], semaphores[n_part + number]
            )
        )
        leaving[number].start()
    for copy in leaving:
        copy.wait()


def finish(total, arrived):
    parts = [one for group in arrived for one in group]
    anywhere = pl.BlockSpec(memory_space=pl.ANY)
    return pl.pallas_call(
        functools.partial(finish_kernel, [len(group) for group in arrived]),
        out_shape=jax.ShapeDtypeStruct(total.shape, jnp.float32),
        in_specs=[pl.BlockSpec(memory_space=pltpu.VMEM)] + [anywhere] * len(parts),
        out_specs=anywhere,
        scratch_shapes=[pltpu.VMEM(total.shape, jnp.float32)]
        + [pltpu.VMEM(part.shape, part.dtype) for part in parts]
        + [pltpu.SemaphoreType.DMA] * (len(parts) + total.shape[0]),
        compiler_params=pltpu.CompilerParams(vmem_limit_bytes=VMEM_LIMIT),
        cost_estimate=pl.CostEstimate(flops=10**9, bytes_accessed=10**7, transcendentals=0),
        name="finish",
    )(total, *parts)


def one_step(normed, segments, scales, lags, n_chan):
    slots = normed.shape[0]
    me = lax.axis_index("chan")
    every = tuple(range(NB))
    arrived = []
    order = ()
    for step in range(n_chan - 1, -1, -1):
        dtype = jnp.bfloat16 if step else jnp.float32
        out = (jax.ShapeDtypeStruct((NB, slots, lags), dtype),)
        place = jnp.stack([me ^ step] * NB)
        order = partial_sums(
            every, write_plain, out, place, normed, segments, scales, order=order
        )
        if step:
            arrived.append(exchange(order[0], step, n_chan))
    total = order[0]
    for part in arrived:
        total = total + part.astype(jnp.float32)
    return total


def body(n_tmpl, n_chan, data, templates, counts, owners):
    lags = LO // n_chan
    parts = [data]
    for step in range(2, n_tmpl, 2):
        parts.append(lax.ppermute(data, "tmpl", [(i, i ^ step) for i in range(n_tmpl)]))
    normed = normalize_templates(counts, templates)
    even, normed = lax.optimization_barrier((jnp.concatenate(parts, 0), normed))
    odd = lax.ppermute(even, "tmpl", [(i, i ^ 1) for i in range(n_tmpl)])
    codes = owners ^ lax.axis_index("tmpl")
    segments, scales = choose_blocks(codes, even, odd)
    if n_chan == 4:
        total = two_steps(normed, segments, scales, lags)
    else:
        total = one_step(normed, segments, scales, lags, n_chan)
    return jnp.transpose(total, (1, 0, 2))


def solution(mesh):
    placed = (P("tmpl", "chan", None), P("tmpl", "chan", None), P("tmpl"), P())
    return jax.shard_map(
        functools.partial(body, mesh.shape["tmpl"], mesh.shape["chan"]),
        mesh=mesh,
        in_specs=placed,
        out_specs=P("tmpl", None, "chan"),
        check_vma=False,
    )
```

```python
import functools
import math

import jax
import jax.numpy as jnp
from jax import lax
from jax.experimental import pallas as pl
from jax.experimental.pallas import tpu as pltpu
from jax.sharding import PartitionSpec as P

W = 200
NB = 3
LO = 2048
TB = 32
EPS = 1e-06
VMEM_LIMIT = 48 * 2**20


def inverse_norm(mean_square):
    return lax.rsqrt(mean_square + EPS) * (1.0 / math.sqrt(W))


def template_kernel(count_ref, tpl_ref, out_ref, scaled_ref):
    chans, _, slots = tpl_ref.shape
    live = lax.broadcasted_iota(jnp.int32, (1, slots), 1) < count_ref[0]
    for c in range(0, chans, 2):
        pair = []
        for k in (c, c + 1):
            values = tpl_ref[k].astype(jnp.float32)
            mean_square = jnp.sum(values * values, axis=0, keepdims=True) * (1.0 / W)
            pair.append(jnp.where(live, values * inverse_norm(mean_square), 0.0))
        scaled_ref[c * W : (c + 2) * W, :] = jnp.concatenate(pair, 0).astype(jnp.bfloat16)
    depth = chans * W
    for at in range(0, depth, slots):
        size = min(slots, depth - at)
        out_ref[:, at : at + size] = scaled_ref[at : at + size, :].T


def normalize_templates(counts, templates):
    slots, chans, _ = templates.shape
    return pl.pallas_call(
        template_kernel,
        out_shape=jax.ShapeDtypeStruct((slots, chans * W), jnp.bfloat16),
        in_specs=[
            pl.BlockSpec(memory_space=pltpu.SMEM),
            pl.BlockSpec(memory_space=pltpu.VMEM),
        ],
        scratch_shapes=[pltpu.VMEM((chans * W, slots), jnp.bfloat16)],
        compiler_params=pltpu.CompilerParams(vmem_limit_bytes=VMEM_LIMIT),
        cost_estimate=pl.CostEstimate(
            flops=4 * slots * chans * W, bytes_accessed=4 * slots * chans * W, transcendentals=0
        ),
        name="normalize_templates",
    )(counts, jnp.transpose(templates, (1, 2, 0)))


def shift_left(x, amount):
    return pltpu.roll(x, x.shape[1] - amount, 1) if amount else x


def block_kernel(code_ref, even_ref, odd_ref, seg_ref, scale_ref):
    chans = even_ref.shape[1]
    lags = scale_ref.shape[2]
    for number in range(NB):
        code = code_ref[number]
        slot = lax.div(code, 2)
        segment = jnp.where(
            lax.rem(code, 2) == 1,
            odd_ref[slot].astype(jnp.float32),
            even_ref[slot].astype(jnp.float32),
        )
        seg_ref[number, :chans, :] = segment.astype(jnp.bfloat16)
        sums = {1: segment * segment}
        for p in range(7):
            sums[2 << p] = sums[1 << p] + shift_left(sums[1 << p], 1 << p)
        total = sums[128] + shift_left(sums[64], 128) + shift_left(sums[8], 192)
        scale_ref[number, :chans, :] = inverse_norm(total[:, :lags] * (1.0 / W))


def choose_blocks(codes, even, odd):
    _, chans, length = even.shape
    held = -(-chans // 8) * 8
    return pl.pallas_call(
        block_kernel,
        out_shape=(
            jax.ShapeDtypeStruct((NB, held, length), jnp.bfloat16),
            jax.ShapeDtypeStruct((NB, held, LO), jnp.float32),
        ),
        in_specs=[
            pl.BlockSpec(memory_space=pltpu.SMEM),
            pl.BlockSpec(memory_space=pltpu.VMEM),
            pl.BlockSpec(memory_space=pltpu.VMEM),
        ],
        compiler_params=pltpu.CompilerParams(vmem_limit_bytes=VMEM_LIMIT),
        cost_estimate=pl.CostEstimate(flops=10**10, bytes_accessed=10**8, transcendentals=0),
        name="choose_blocks",
    )(codes, even, odd)


def build_windows(at, held, chans, base_ref, scale_ref, win_ref):
    lags = win_ref.shape[1]
    tiles = base_ref.shape[0]
    scale = scale_ref[at * held : (at + 1) * held, :]
    for c in range(0, chans, 2):
        rows = []
        for k in (c, c + 1):
            line = (at * held + k) * 8
            base = jnp.concatenate([base_ref[j, line : line + 8, :] for j in range(tiles)], 1)
            row_scale = jnp.broadcast_to(scale[k : k + 1, :], (8, lags))
            wide = [shift_left(base, 8 * g)[:, : lags + 128] for g in range(16)]
            rows += [wide[g][:, :lags] * row_scale for g in range(16)]
            rows += [wide[g][:, 128:] * row_scale for g in range((W - 128) // 8)]
        win_ref[c * W : (c + 2) * W, :] = jnp.concatenate(rows, 0).astype(jnp.bfloat16)


def partial_kernel(chunks, n_add, n_order, write, place_ref, tpl_ref, seg_ref, scale_ref, *refs):
    adds, outs = refs[:n_add], refs[n_add + n_order : -4]
    seg_now, scale_now, base_now, win_ref = refs[-4:]
    depth, lags = win_ref.shape
    held = seg_ref.shape[1]
    span = seg_now.shape[1]
    for index, number in enumerate(chunks):
        start = pl.multiple_of(place_ref[index] * lags, 128)
        lines = slice(index * held, (index + 1) * held)
        seg_now[lines, :] = seg_ref[number, :, pl.ds(start, span)].astype(jnp.float32)
        scale_now[lines, :] = scale_ref[number, :, pl.ds(start, lags)]
    segment = seg_now[...]
    for s in range(8):
        moved = shift_left(segment, s)
        for j in range(span // 128):
            base_now[j, pl.ds(s, segment.shape[0], stride=8), :] = moved[:, 128 * j : 128 * (j + 1)]
    for index in range(len(chunks)):
        build_windows(index, held, depth // W, base_now, scale_now, win_ref)
        product = jnp.dot(tpl_ref[...], win_ref[...], preferred_element_type=jnp.float32)
        write(index, product, adds, outs)


def partial_sums(chunks, write, outs, place, normed, segments, scales, adds=(), order=()):
    lags = outs[0].shape[-1]
    depth = normed.shape[1]
    held = segments.shape[1]
    whole = pl.BlockSpec(memory_space=pltpu.VMEM)
    return pl.pallas_call(
        functools.partial(partial_kernel, chunks, len(adds), len(order), write),
        out_shape=outs,
        in_specs=[
            pl.BlockSpec(memory_space=pltpu.SMEM),
            whole,
            whole,
            whole,
        ]
        + [whole] * len(adds)
        + [pl.BlockSpec(memory_space=pl.ANY)] * len(order),
        scratch_shapes=[
            pltpu.VMEM((len(chunks) * held, lags + 256), jnp.float32),
            pltpu.VMEM((len(chunks) * held, lags), jnp.float32),
            pltpu.VMEM(((lags + 256) // 128, len(chunks) * held * 8, 128), jnp.float32),
            pltpu.VMEM((depth, lags), jnp.bfloat16),
        ],
        compiler_params=pltpu.CompilerParams(vmem_limit_bytes=VMEM_LIMIT),
        cost_estimate=pl.CostEstimate(flops=10**12, bytes_accessed=10**10, transcendentals=0),
        name="partial_sums",
    )(place, normed, segments, scales, *adds, *order)


def write_plain(index, product, adds, outs):
    if len(outs) == 1:
        outs[0][index] = product.astype(outs[0].dtype)
    else:
        outs[index][...] = product.astype(outs[index].dtype)


def write_across(index, product, adds, outs):
    half = outs[0].shape[1]
    if index < outs[0].shape[0]:
        outs[0][index] = product[:half].astype(jnp.bfloat16)
        outs[1][index] = product[half:].astype(jnp.bfloat16)
    else:
        outs[2][...] = product.astype(jnp.bfloat16)


def write_added(at, index, product, adds, outs):
    half = product.shape[0] // 2
    here = adds[index][at].astype(jnp.float32)
    if index == 0:
        outs[0][:half] = product[:half].astype(jnp.bfloat16)
        outs[0][half:] = (product[half:] + here).astype(jnp.bfloat16)
    else:
        outs[1][:half] = (product[:half] + here).astype(jnp.bfloat16)
        outs[1][half:] = product[half:].astype(jnp.bfloat16)


def exchange(value, step, n_chan):
    return lax.ppermute(value, "chan", [(i, i ^ step) for i in range(n_chan)])


def two_steps(normed, segments, scales, lags):
    slots = normed.shape[0]
    me = lax.axis_index("chan")
    args = (normed, segments, scales)

    def message(*shape):
        return jax.ShapeDtypeStruct(shape + (lags,), jnp.bfloat16)

    upper, lower, far = partial_sums(
        (1, 2, 0),
        write_across,
        (message(2, slots // 2), message(2, slots // 2), message(slots)),
        jnp.stack([me ^ 3] * NB),
        *args,
    )
    via_x, via_y = exchange(upper, 1, 4), exchange(lower, 2, 4)
    straight = exchange(far, 3, 4)
    arrived = []
    place = jnp.stack([me ^ 1, me ^ 2])
    order = (far,)
    for number in range(NB):
        write, adds = write_plain, ()
        if number > 0:
            write, adds = functools.partial(write_added, number - 1), (via_y, via_x)
        to_x, to_y = partial_sums(
            (number, number), write, (message(slots),) * 2, place, *args, adds=adds, order=order
        )
        order = (to_y,)
        if number == 1:
            order += (straight,)
        if number == NB - 1:
            to_x, to_y, *first = lax.optimization_barrier((to_x, to_y, *arrived[0]))
            arrived[0] = tuple(first)
        arrived.append((exchange(to_x, 1, 4), exchange(to_y, 2, 4)))
    totals = []
    order = order[:1]
    for chunks in ((0,), (1, 2)):
        totals += partial_sums(
            chunks,
            write_plain,
            (jax.ShapeDtypeStruct((len(chunks), slots, lags), jnp.float32),),
            jnp.stack([me] * len(chunks)),
            *args,
            order=order,
        )
        order = (totals[0], *arrived[1])
    arrived[0] += (straight,)
    return finish(totals, arrived)


def finish_kernel(shares, first_ref, rest_ref, *refs):
    n_part = sum(shares)
    parts, out_ref, stage = refs[:n_part], refs[n_part], refs[n_part + 1]
    held = refs[n_part + 2 : 2 * n_part + 2]
    semaphores = refs[2 * n_part + 2 :]
    arriving = [pltpu.make_async_copy(*trio) for trio in zip(parts, held, semaphores)]
    for copy in arriving:
        copy.start()
    leaving = []
    at = 0
    for number, share in enumerate(shares):
        value = rest_ref[number - 1] if number else first_ref[0]
        for index in range(at, at + share):
            arriving[index].wait()
            value = value + held[index][...].astype(jnp.float32)
        at += share
        stage[number] = value
        leaving.append(
            pltpu.make_async_copy(
                stage.at[number], out_ref.at[number], semaphores[n_part + number]
            )
        )
        leaving[number].start()
    for copy in leaving:
        copy.wait()


def finish(totals, arrived):
    parts = [one for group in arrived for one in group]
    shape = (NB,) + totals[0].shape[1:]
    whole = pl.BlockSpec(memory_space=pltpu.VMEM)
    anywhere = pl.BlockSpec(memory_space=pl.ANY)
    return pl.pallas_call(
        functools.partial(finish_kernel, [len(group) for group in arrived]),
        out_shape=jax.ShapeDtypeStruct(shape, jnp.float32),
        in_specs=[whole, whole] + [anywhere] * len(parts),
        out_specs=anywhere,
        scratch_shapes=[pltpu.VMEM(shape, jnp.float32)]
        + [pltpu.VMEM(part.shape, part.dtype) for part in parts]
        + [pltpu.SemaphoreType.DMA] * (len(parts) + NB),
        compiler_params=pltpu.CompilerParams(vmem_limit_bytes=VMEM_LIMIT),
        cost_estimate=pl.CostEstimate(flops=10**9, bytes_accessed=10**7, transcendentals=0),
        name="finish",
    )(*totals, *parts)


def one_step(normed, segments, scales, lags, n_chan):
    slots = normed.shape[0]
    me = lax.axis_index("chan")
    every = tuple(range(NB))
    arrived = []
    order = ()
    for step in range(n_chan - 1, -1, -1):
        dtype = jnp.bfloat16 if step else jnp.float32
        out = (jax.ShapeDtypeStruct((NB, slots, lags), dtype),)
        place = jnp.stack([me ^ step] * NB)
        order = partial_sums(
            every, write_plain, out, place, normed, segments, scales, order=order
        )
        if step:
            arrived.append(exchange(order[0], step, n_chan))
    total = order[0]
    for part in arrived:
        total = total + part.astype(jnp.float32)
    return total


def body(n_tmpl, n_chan, data, templates, counts, owners):
    lags = LO // n_chan
    parts = [data]
    for step in range(2, n_tmpl, 2):
        parts.append(lax.ppermute(data, "tmpl", [(i, i ^ step) for i in range(n_tmpl)]))
    normed = normalize_templates(counts, templates)
    even, normed = lax.optimization_barrier((jnp.concatenate(parts, 0), normed))
    odd = lax.ppermute(even, "tmpl", [(i, i ^ 1) for i in range(n_tmpl)])
    codes = owners ^ lax.axis_index("tmpl")
    segments, scales = choose_blocks(codes, even, odd)
    if n_chan == 4:
        total = two_steps(normed, segments, scales, lags)
    else:
        total = one_step(normed, segments, scales, lags, n_chan)
    return jnp.transpose(total, (1, 0, 2))


def solution(mesh):
    placed = (P("tmpl", "chan", None), P("tmpl", "chan", None), P("tmpl"), P())
    return jax.shard_map(
        functools.partial(body, mesh.shape["tmpl"], mesh.shape["chan"]),
        mesh=mesh,
        in_specs=placed,
        out_specs=P("tmpl", None, "chan"),
        check_vma=False,
    )
```

```python
import functools
import math

import jax
import jax.numpy as jnp
from jax import lax
from jax.experimental import pallas as pl
from jax.experimental.pallas import tpu as pltpu
from jax.sharding import PartitionSpec as P

W = 200
NB = 3
LO = 2048
TB = 32
EPS = 1e-06
VMEM_LIMIT = 48 * 2**20


def inverse_norm(mean_square):
    return lax.rsqrt(mean_square + EPS) * (1.0 / math.sqrt(W))


def template_kernel(count_ref, tpl_ref, out_ref, scaled_ref):
    chans, _, slots = tpl_ref.shape
    live = lax.broadcasted_iota(jnp.int32, (1, slots), 1) < count_ref[0]
    for c in range(0, chans, 2):
        pair = []
        for k in (c, c + 1):
            values = tpl_ref[k].astype(jnp.float32)
            mean_square = jnp.sum(values * values, axis=0, keepdims=True) * (1.0 / W)
            pair.append(jnp.where(live, values * inverse_norm(mean_square), 0.0))
        scaled_ref[c * W : (c + 2) * W, :] = jnp.concatenate(pair, 0).astype(jnp.bfloat16)
    depth = chans * W
    for at in range(0, depth, slots):
        size = min(slots, depth - at)
        out_ref[:, at : at + size] = scaled_ref[at : at + size, :].T


def normalize_templates(counts, templates):
    slots, chans, _ = templates.shape
    return pl.pallas_call(
        template_kernel,
        out_shape=jax.ShapeDtypeStruct((slots, chans * W), jnp.bfloat16),
        in_specs=[
            pl.BlockSpec(memory_space=pltpu.SMEM),
            pl.BlockSpec(memory_space=pltpu.VMEM),
        ],
        scratch_shapes=[pltpu.VMEM((chans * W, slots), jnp.bfloat16)],
        compiler_params=pltpu.CompilerParams(vmem_limit_bytes=VMEM_LIMIT),
        cost_estimate=pl.CostEstimate(
            flops=4 * slots * chans * W, bytes_accessed=4 * slots * chans * W, transcendentals=0
        ),
        name="normalize_templates",
    )(counts, jnp.transpose(templates, (1, 2, 0)))


def shift_left(x, amount):
    return pltpu.roll(x, x.shape[1] - amount, 1) if amount else x


def block_kernel(code_ref, even_ref, odd_ref, seg_ref, scale_ref):
    chans = even_ref.shape[1]
    lags = scale_ref.shape[2]
    for number in range(NB):
        code = code_ref[number]
        slot = lax.div(code, 2)
        segment = jnp.where(
            lax.rem(code, 2) == 1,
            odd_ref[slot].astype(jnp.float32),
            even_ref[slot].astype(jnp.float32),
        )
        seg_ref[number, :chans, :] = segment.astype(jnp.bfloat16)
        sums = {1: segment * segment}
        for p in range(7):
            sums[2 << p] = sums[1 << p] + shift_left(sums[1 << p], 1 << p)
        total = sums[128] + shift_left(sums[64], 128) + shift_left(sums[8], 192)
        scale_ref[number, :chans, :] = inverse_norm(total[:, :lags] * (1.0 / W))


def choose_blocks(codes, even, odd):
    _, chans, length = even.shape
    held = -(-chans // 8) * 8
    return pl.pallas_call(
        block_kernel,
        out_shape=(
            jax.ShapeDtypeStruct((NB, held, length), jnp.bfloat16),
            jax.ShapeDtypeStruct((NB, held, LO), jnp.float32),
        ),
        in_specs=[
            pl.BlockSpec(memory_space=pltpu.SMEM),
            pl.BlockSpec(memory_space=pltpu.VMEM),
            pl.BlockSpec(memory_space=pltpu.VMEM),
        ],
        compiler_params=pltpu.CompilerParams(vmem_limit_bytes=VMEM_LIMIT),
        cost_estimate=pl.CostEstimate(flops=10**10, bytes_accessed=10**8, transcendentals=0),
        name="choose_blocks",
    )(codes, even, odd)


def build_windows(at, held, chans, base_ref, scale_ref, win_ref):
    lags = win_ref.shape[1]
    tiles = base_ref.shape[0]
    scale = scale_ref[at * held : (at + 1) * held, :]
    for c in range(0, chans, 2):
        rows = []
        for k in (c, c + 1):
            line = (at * held + k) * 8
            base = jnp.concatenate([base_ref[j, line : line + 8, :] for j in range(tiles)], 1)
            row_scale = jnp.broadcast_to(scale[k : k + 1, :], (8, lags))
            wide = [shift_left(base, 8 * g)[:, : lags + 128] for g in range(16)]
            rows += [wide[g][:, :lags] * row_scale for g in range(16)]
            rows += [wide[g][:, 128:] * row_scale for g in range((W - 128) // 8)]
        win_ref[c * W : (c + 2) * W, :] = jnp.concatenate(rows, 0).astype(jnp.bfloat16)


def partial_kernel(chunks, n_add, n_order, write, place_ref, tpl_ref, seg_ref, scale_ref, *refs):
    adds, outs = refs[:n_add], refs[n_add + n_order : -4]
    seg_now, scale_now, base_now, win_ref = refs[-4:]
    depth, lags = win_ref.shape
    held = seg_ref.shape[1]
    span = seg_now.shape[1]
    for index, number in enumerate(chunks):
        start = pl.multiple_of(place_ref[index] * lags, 128)
        lines = slice(index * held, (index + 1) * held)
        seg_now[lines, :] = seg_ref[number, :, pl.ds(start, span)].astype(jnp.float32)
        scale_now[lines, :] = scale_ref[number, :, pl.ds(start, lags)]
    segment = seg_now[...]
    for s in range(8):
        moved = shift_left(segment, s)
        for j in range(span // 128):
            base_now[j, pl.ds(s, segment.shape[0], stride=8), :] = moved[:, 128 * j : 128 * (j + 1)]
    for index in range(len(chunks)):
        build_windows(index, held, depth // W, base_now, scale_now, win_ref)
        product = jnp.dot(tpl_ref[...], win_ref[...], preferred_element_type=jnp.float32)
        write(index, product, adds, outs)


def partial_sums(chunks, write, outs, place, normed, segments, scales, adds=(), order=()):
    lags = outs[0].shape[-1]
    depth = normed.shape[1]
    held = segments.shape[1]
    whole = pl.BlockSpec(memory_space=pltpu.VMEM)
    return pl.pallas_call(
        functools.partial(partial_kernel, chunks, len(adds), len(order), write),
        out_shape=outs,
        in_specs=[
            pl.BlockSpec(memory_space=pltpu.SMEM),
            whole,
            whole,
            whole,
        ]
        + [whole] * len(adds)
        + [pl.BlockSpec(memory_space=pl.ANY)] * len(order),
        scratch_shapes=[
            pltpu.VMEM((len(chunks) * held, lags + 256), jnp.float32),
            pltpu.VMEM((len(chunks) * held, lags), jnp.float32),
            pltpu.VMEM(((lags + 256) // 128, len(chunks) * held * 8, 128), jnp.float32),
            pltpu.VMEM((depth, lags), jnp.bfloat16),
        ],
        compiler_params=pltpu.CompilerParams(vmem_limit_bytes=VMEM_LIMIT),
        cost_estimate=pl.CostEstimate(flops=10**12, bytes_accessed=10**10, transcendentals=0),
        name="partial_sums",
    )(place, normed, segments, scales, *adds, *order)


def write_plain(index, product, adds, outs):
    if len(outs) == 1:
        outs[0][index] = product.astype(outs[0].dtype)
    else:
        outs[index][...] = product.astype(outs[index].dtype)


def write_across(index, product, adds, outs):
    half = outs[0].shape[1]
    if index < outs[0].shape[0]:
        outs[0][index] = product[:half].astype(jnp.bfloat16)
        outs[1][index] = product[half:].astype(jnp.bfloat16)
    else:
        outs[2][...] = product.astype(jnp.bfloat16)


def write_added(at, index, product, adds, outs):
    half = product.shape[0] // 2
    here = adds[index][at].astype(jnp.float32)
    if index == 0:
        outs[0][:half] = product[:half].astype(jnp.bfloat16)
        outs[0][half:] = (product[half:] + here).astype(jnp.bfloat16)
    else:
        outs[1][:half] = (product[:half] + here).astype(jnp.bfloat16)
        outs[1][half:] = product[half:].astype(jnp.bfloat16)


def exchange(value, step, n_chan):
    return lax.ppermute(value, "chan", [(i, i ^ step) for i in range(n_chan)])


def two_steps(normed, segments, scales, lags):
    slots = normed.shape[0]
    me = lax.axis_index("chan")
    args = (normed, segments, scales)

    def message(*shape):
        return jax.ShapeDtypeStruct(shape + (lags,), jnp.bfloat16)

    upper, lower, far = partial_sums(
        (1, 2, 0),
        write_across,
        (message(2, slots // 2), message(2, slots // 2), message(slots)),
        jnp.stack([me ^ 3] * NB),
        *args,
    )
    via_x, via_y = exchange(upper, 1, 4), exchange(lower, 2, 4)
    straight = exchange(far, 3, 4)
    arrived = []
    place = jnp.stack([me ^ 1, me ^ 2])
    order = (far,)
    for number in range(NB):
        write, adds = write_plain, ()
        if number > 0:
            write, adds = functools.partial(write_added, number - 1), (via_y, via_x)
        to_x, to_y = partial_sums(
            (number, number), write, (message(slots),) * 2, place, *args, adds=adds, order=order
        )
        order = (to_y,)
        if number == 1:
            order += (straight,)
        if number == NB - 1:
            to_x, to_y, *first = lax.optimization_barrier((to_x, to_y, *arrived[0]))
            arrived[0] = tuple(first)
        arrived.append((exchange(to_x, 1, 4), exchange(to_y, 2, 4)))
    totals = []
    order = order[:1]
    for chunks in ((0,), (1, 2)):
        totals += partial_sums(
            chunks,
            write_plain,
            (jax.ShapeDtypeStruct((len(chunks), slots, lags), jnp.float32),),
            jnp.stack([me] * len(chunks)),
            *args,
            order=order,
        )
        order = (totals[0], *arrived[1])
    arrived[0] += (straight,)
    return finish(totals, arrived)


def finish_kernel(shares, first_ref, rest_ref, *refs):
    n_part = sum(shares)
    parts, out_ref, stage = refs[:n_part], refs[n_part], refs[n_part + 1]
    held = refs[n_part + 2 : 2 * n_part + 2]
    semaphores = refs[2 * n_part + 2 :]
    arriving = [pltpu.make_async_copy(*trio) for trio in zip(parts, held, semaphores)]
    for copy in arriving:
        copy.start()
    bases = [
        pltpu.make_async_copy(first_ref, stage.at[:1], semaphores[-2]),
        pltpu.make_async_copy(rest_ref, stage.at[1:], semaphores[-1]),
    ]
    for copy in bases:
        copy.start()
    leaving = []
    at = 0
    for number, share in enumerate(shares):
        if number < 2:
            bases[number].wait()
        value = stage[number]
        for index in range(at, at + share):
            arriving[index].wait()
            value = value + held[index][...].astype(jnp.float32)
        at += share
        stage[number] = value
        leaving.append(
            pltpu.make_async_copy(
                stage.at[number], out_ref.at[number], semaphores[n_part + number]
            )
        )
        leaving[number].start()
    for copy in leaving:
        copy.wait()


def finish(totals, arrived):
    parts = [one for group in arrived for one in group]
    shape = (NB,) + totals[0].shape[1:]
    anywhere = pl.BlockSpec(memory_space=pl.ANY)
    return pl.pallas_call(
        functools.partial(finish_kernel, [len(group) for group in arrived]),
        out_shape=jax.ShapeDtypeStruct(shape, jnp.float32),
        in_specs=[anywhere, anywhere] + [anywhere] * len(parts),
        out_specs=anywhere,
        scratch_shapes=[pltpu.VMEM(shape, jnp.float32)]
        + [pltpu.VMEM(part.shape, part.dtype) for part in parts]
        + [pltpu.SemaphoreType.DMA] * (len(parts) + NB + 2),
        compiler_params=pltpu.CompilerParams(vmem_limit_bytes=VMEM_LIMIT),
        cost_estimate=pl.CostEstimate(flops=10**9, bytes_accessed=10**7, transcendentals=0),
        name="finish",
    )(*totals, *parts)


def one_step(normed, segments, scales, lags, n_chan):
    slots = normed.shape[0]
    me = lax.axis_index("chan")
    every = tuple(range(NB))
    arrived = []
    order = ()
    for step in range(n_chan - 1, -1, -1):
        dtype = jnp.bfloat16 if step else jnp.float32
        out = (jax.ShapeDtypeStruct((NB, slots, lags), dtype),)
        place = jnp.stack([me ^ step] * NB)
        order = partial_sums(
            every, write_plain, out, place, normed, segments, scales, order=order
        )
        if step:
            arrived.append(exchange(order[0], step, n_chan))
    total = order[0]
    for part in arrived:
        total = total + part.astype(jnp.float32)
    return total


def body(n_tmpl, n_chan, data, templates, counts, owners):
    lags = LO // n_chan
    parts = [data]
    for step in range(2, n_tmpl, 2):
        parts.append(lax.ppermute(data, "tmpl", [(i, i ^ step) for i in range(n_tmpl)]))
    normed = normalize_templates(counts, templates)
    even, normed = lax.optimization_barrier((jnp.concatenate(parts, 0), normed))
    odd = lax.ppermute(even, "tmpl", [(i, i ^ 1) for i in range(n_tmpl)])
    codes = owners ^ lax.axis_index("tmpl")
    segments, scales = choose_blocks(codes, even, odd)
    if n_chan == 4:
        total = two_steps(normed, segments, scales, lags)
    else:
        total = one_step(normed, segments, scales, lags, n_chan)
    return jnp.transpose(total, (1, 0, 2))


def solution(mesh):
    placed = (P("tmpl", "chan", None), P("tmpl", "chan", None), P("tmpl"), P())
    return jax.shard_map(
        functools.partial(body, mesh.shape["tmpl"], mesh.shape["chan"]),
        mesh=mesh,
        in_specs=placed,
        out_specs=P("tmpl", None, "chan"),
        check_vma=False,
    )
```
